256 devices in a mesh: pair: 32 (over y, z_lo, core), win: 8 (over x, z_hi).
Axes of the slice: x: 4, y: 4, z: 8 (z_hi: 2, z_lo: 4; z = z_hi * 4 + z_lo), core: 2. Of those that a mesh axis runs over, the one named last changes fastest.
Arguments:
- traces: bfloat16 [4096, 256, 1024], P('pair', 'win'), may hold values from -6 to 6
- taps: float32 [64], replicated, may hold values from -0.5 to 0.5
- alive: int32 [4096], P('pair'), may hold values 0 or 1
Outputs:
- cross: bfloat16 [2, 2, 256, 4096, 128], P(None, None, 'win', 'pair')
The draws below stay inside these ranges and needn't reach their ends.
All inputs are finite; a program needn't handle non-finite values. No bound on the sum of `alive` on one device may be relied on, other than what follows from the above.
Results may differ from the reference program's by a relative error of at most 0.0071.
Values may be sent and summed in bfloat16 or wider, within the bound.
A program may use at most 128 MiB of HBM per device.

```python
import math
import jax
import jax.numpy as jnp
from jax import lax

CH_DEV = 128
SAMPLES = 1024
BINS = 256
TAPS = 64
CHANNELS = 4096
SUBWIN = 256
N_PAIR = 32


def plant(drawn, key, low, high):
    place = [jax.random.randint(jax.random.fold_in(key, axis), (), 0, length) for axis, length in enumerate(drawn.shape)]
    widest = drawn.shape.index(max(drawn.shape))
    neighbour = place[:widest] + [(place[widest] + 1) % drawn.shape[widest]] + place[widest + 1:]
    return drawn.at[tuple(place)].set(low).at[tuple(neighbour)].set(high)


def shard_levels(own_key, shape, pieces, least, high):
    def one(dim, blocks):
        heights = jax.random.uniform(jax.random.fold_in(jax.random.fold_in(own_key, 6), dim), (blocks,), jnp.float32, least / len(pieces), high / len(pieces))
        return jnp.repeat(jnp.exp(heights), shape[dim] // blocks).reshape((-1,) + (1,) * (len(shape) - dim - 1))

    gain = one(*pieces[0])
    for cut in pieces[1:]:
        gain = gain * one(*cut)
    return gain


def scatter_about(rng, dims, width, most, cuts=(), kind=jnp.bfloat16):
    entries = width * jax.random.normal(rng, dims, jnp.float32)
    if cuts:
        entries = entries * shard_levels(rng, dims, cuts, -0.22, 0.18)
    return jnp.clip(entries, -most, most).astype(kind)


def setup_inputs(seed: int = 0) -> dict:
    keys = jax.random.split(jax.random.key(seed), 4)
    traces = scatter_about(keys[0], (CHANNELS, SUBWIN, SAMPLES), 1.0, 6.0, ((0, 32), (1, 8)))
    taps = scatter_about(keys[1], (TAPS,), 0.125, 0.5, (), jnp.float32)
    alive = plant((jax.random.randint(keys[2], (CHANNELS,), 0, 8) < 7).astype(jnp.int32), jax.random.fold_in(keys[2], 1), 0, 1)
    return {"traces": traces, "taps": taps, "alive": alive}


def filtered_basis(taps, samples, bins):
    ntaps = taps.shape[0]
    length = samples + ntaps
    sample_index = jnp.arange(samples, dtype=jnp.int32)[:, None]
    bin_index = jnp.arange(bins, dtype=jnp.int32)[None, :]
    phase = (sample_index * bin_index % samples).astype(jnp.float32) * (2.0 * math.pi / samples)
    scale = 1.0 / math.sqrt(samples)
    plain = jnp.concatenate([jnp.cos(phase), -jnp.sin(phase)], axis=1) * scale
    period = 2 * samples + ntaps
    pattern = jnp.concatenate([jnp.zeros((period - ntaps,), jnp.float32), taps.astype(jnp.float32)])
    tiled = jnp.tile(pattern, length)[:length * (period - 1)]
    filt = tiled.reshape(length, period - 1)[:, :samples]
    total = jnp.dot(filt, plain, preferred_element_type=jnp.float32, precision=lax.Precision.HIGHEST)
    return total.astype(jnp.bfloat16)

def reference(traces, taps, alive):
    basis = filtered_basis(taps, SAMPLES, BINS)
    length = SAMPLES + TAPS
    blocks = traces.reshape(N_PAIR, CH_DEV, SUBWIN, SAMPLES)
    alive_blocks = alive.reshape(N_PAIR, CH_DEV)
    prev_blocks = jnp.concatenate([jnp.zeros((N_PAIR, CH_DEV, 1, SAMPLES), jnp.bfloat16), blocks[:, :, :-1, :]], axis=2)

    def block_spectra(items):
        record, before, alive_rows = items
        extended = jnp.concatenate([before[:, :, SAMPLES - TAPS:], record], axis=2)
        product = jnp.dot(extended.reshape(CH_DEV * SUBWIN, length), basis, preferred_element_type=jnp.float32)
        product = product.reshape(CH_DEV, SUBWIN, 2 * BINS) * alive_rows.astype(jnp.float32)[:, None, None]
        return product.astype(jnp.bfloat16)
    spectra = lax.map(block_spectra, (blocks, prev_blocks, alive_blocks))
    norm = 1.0 / math.sqrt(SUBWIN)

    def block_cross(items):
        mine, other = items
        mine_re = mine[:, :, :BINS].astype(jnp.float32)
        mine_im = mine[:, :, BINS:].astype(jnp.float32)
        other_re = other[:, :, :BINS].astype(jnp.float32)
        other_im = other[:, :, BINS:].astype(jnp.float32)
        real_part = jnp.einsum('isf,jsf->fij', mine_re, other_re) + jnp.einsum('isf,jsf->fij', mine_im, other_im)
        imag_part = jnp.einsum('isf,jsf->fij', mine_im, other_re) - jnp.einsum('isf,jsf->fij', mine_re, other_im)
        return (jnp.stack([real_part, imag_part], 0) * norm).astype(jnp.bfloat16)
    rounds = []
    for offset in (1, N_PAIR // 2):
        partner = jnp.roll(spectra, offset, axis=0)
        result = lax.map(block_cross, (spectra, partner))
        result = jnp.transpose(result, (1, 2, 0, 3, 4)).reshape(2, BINS, CHANNELS, CH_DEV)
        rounds.append(result)
    return jnp.stack(rounds, axis=1)
```

```python
import math

import jax
import jax.numpy as jnp
import numpy as np
from jax import lax
from jax.experimental import pallas as pl
from jax.experimental.pallas import tpu as pltpu
from jax.sharding import PartitionSpec as P

BINS = 256
SHARE = 32
CH = 128
SUBS = 32
SAMPLES = 1024
TAPS = 64
CHUNKS = 4
PER = SHARE // CHUNKS
MESH = pl.DeviceIdType.MESH
F32 = jnp.float32
BF16 = jnp.bfloat16
NT = (((1,), (1,)), ((), ()))
TN = (((0,), (0,)), ((), ()))


def tables():
    k = np.arange(BINS)[:, None]
    n = np.arange(SAMPLES)[None, :]
    phase = ((k * n) % SAMPLES) * (2.0 * math.pi / SAMPLES)
    return np.cos(phase).astype(np.float32), np.sin(phase).astype(np.float32)


def gather_matrix():
    m = np.zeros((256, 256), np.float32)
    for s in range(16):
        for ch in range(16):
            m[s * 16 + ch, ch * 16 + s] = 1.0
    return m


PIECES = ["own", 0, 1, 2, 3]


def part(ref, piece):
    if piece == "own":
        return ref.at[:, pl.ds(0, SUBS), :]
    return ref.at[pl.ds(PER * piece, PER), pl.ds(SUBS, 3 * SUBS), :]


def peers(ref, piece):
    return ref.at[pl.ds(PER * piece, PER)]


def sem_table():
    names = ["tail"]
    names += [("x", half, r, j) for half in (0, 1) for j in range(CHUNKS) for r in (1, 2, 3)]
    for kind in ("swap", "relay", "pass", "near", "far", "ynear", "yfar"):
        names += [(kind, piece) for piece in PIECES]
    return {name: i for i, name in enumerate(names)}


SEMS = sem_table()


def kernel(
    traces, taps, alive, cos_hbm, sin_hbm, perm, out,
    tv, ts, cosv, sinv, basis, acc, sp, own, pb0, pb1, swp, rly, rlp, outv,
    load_sem, out_sem, send_sem, recv_sem,
):
    pair, win = lax.axis_index("pair"), lax.axis_index("win")
    c, zl, y = lax.rem(pair, 2), lax.rem(pair // 2, 4), pair // 8
    x, hz = win // 2, lax.rem(win, 2)
    z = hz * 4 + zl

    def dev(dx, dy, dz, core):
        xx, yy, zz = lax.rem(x + dx + 4, 4), lax.rem(y + dy + 4, 4), lax.rem(z + dz + 8, 8)
        return {"pair": (yy * 4 + lax.rem(zz, 4)) * 2 + core, "win": xx * 2 + zz // 4}

    last = jnp.where(zl == 3, 1, 0)
    first = jnp.where(zl == 0, 1, 0)
    next_win = {"pair": pair, "win": lax.rem(win + 1, 8)}
    prev_win = {"pair": pair, "win": lax.rem(win + 7, 8)}
    swap_to = dev(0, last, -3 + 4 * last, 0)
    near_to = dev(0, last, 1 - 4 * last, 0)
    swap_from = dev(0, -first, 3 - 4 * first, 1)
    near_from = dev(0, -first, -1 + 4 * first, 1)

    barrier = pltpu.get_barrier_semaphore()
    same = [dev(r, 0, 0, c) for r in (1, 2, 3)] + [next_win, prev_win]
    same += [dev(0, 0, 2, c), dev(0, 0, -2, c), dev(0, 2, 0, c), dev(0, 0, 0, 1 - c)]
    for target in same:
        pl.semaphore_signal(barrier, inc=1, device_id=target, device_id_type=MESH)

    @pl.when(c == 0)
    def _():
        for target in (swap_from, near_from):
            pl.semaphore_signal(barrier, inc=1, device_id=target, device_id_type=MESH)

    @pl.when(c == 1)
    def _():
        for target in (swap_to, near_to):
            pl.semaphore_signal(barrier, inc=1, device_id=target, device_id_type=MESH)

    copies = [
        pltpu.make_async_copy(cos_hbm, cosv, load_sem.at[8]),
        pltpu.make_async_copy(sin_hbm, sinv, load_sem.at[9]),
    ]
    for copy in copies:
        copy.start()

    def load(g):
        rows = pl.ds(pl.multiple_of(g * 16, 16), 16)
        return pltpu.make_async_copy(traces.at[rows], tv.at[rows], load_sem.at[g])

    for g in range(8):
        load(g).start()
    for copy in copies:
        copy.wait()

    scale = 1.0 / math.sqrt(SAMPLES)
    tap_row = taps[0:1, :]
    lanes = lax.broadcasted_iota(jnp.int32, (128, 128), 1)
    rows = lax.broadcasted_iota(jnp.int32, (128, 128), 0)
    turned = pltpu.roll(jnp.broadcast_to(tap_row, (128, 128)), 0, 1, stride=1, stride_axis=0)
    edge = jnp.where((rows >= TAPS) & (lanes < rows - TAPS), turned, 0.0)
    for half in (0, 1):
        h = hz if half else 1 - hz
        for r in range(4):
            k0 = pl.multiple_of(SHARE * (2 * lax.rem(x + r, 4) + h), SHARE)
            head_cos = cosv[pl.ds(k0, SHARE), 0:128]
            head_sin = sinv[pl.ds(k0, SHARE), 0:128]
            hr = jnp.sum(head_cos * tap_row, axis=1, keepdims=True) * scale
            hi = -jnp.sum(head_sin * tap_row, axis=1, keepdims=True) * scale
            left_re = lax.dot_general(
                head_cos * scale, edge, NT, precision=lax.Precision.HIGHEST, preferred_element_type=F32
            )
            left_im = lax.dot_general(
                head_sin * -scale, edge, NT, precision=lax.Precision.HIGHEST, preferred_element_type=F32
            )
            for t in range(8):
                cs = cosv[pl.ds(k0, SHARE), 128 * t : 128 * t + 128]
                sn = sinv[pl.ds(k0, SHARE), 128 * t : 128 * t + 128]
                re = cs * hr + sn * hi
                im = cs * hi - sn * hr
                if t == 7:
                    re = re - left_re
                    im = im - left_im
                basis[half, 64 * r : 64 * r + 32, 128 * t : 128 * t + 128] = re.astype(BF16)
                basis[half, 64 * r + 32 : 64 * r + 64, 128 * t : 128 * t + 128] = im.astype(BF16)
            basis[half, 64 * r : 64 * r + 32, 1024:1152] = left_re.astype(BF16)
            basis[half, 64 * r + 32 : 64 * r + 64, 1024:1152] = left_im.astype(BF16)

    def regroup(g, carry):
        load(g).wait()
        chans = pl.ds(pl.multiple_of(g * 16, 16), 16)
        for sh in (0, 1):
            for t in range(4):
                cols = slice(256 * t, 256 * t + 256)
                block = tv[chans, 16 * sh : 16 * sh + 16, cols].reshape(256, 256)
                moved = jnp.dot(perm[...], block, preferred_element_type=F32).astype(BF16)
                ts[pl.ds(1 + 16 * sh, 16), chans, cols] = moved.reshape(16, 16, 256)
        return carry

    lax.fori_loop(0, 8, regroup, 0)

    pl.semaphore_wait(barrier, 11)

    def remote(name, src, dst, target, sent=None):
        return pltpu.make_async_remote_copy(
            src_ref=src, dst_ref=dst, send_sem=send_sem.at[SEMS[sent or name]], recv_sem=recv_sem.at[SEMS[name]],
            device_id=target, device_id_type=MESH,
        )

    tail = remote("tail", ts.at[SUBS, :, pl.ds(896, 128)], ts.at[0, :, pl.ds(896, 128)], next_win)
    tail.start()

    alive_row = jnp.concatenate([alive[0:1, :], alive[0:1, :]], axis=1)

    def transform(half, p):
        s0 = p * 2
        main = ts[pl.ds(s0 + 1, 2)].reshape(256, SAMPLES)
        prior = ts[pl.ds(s0, 2), :, 896:1024].reshape(256, 128)
        total = lax.dot_general(basis[half, :, 0:1024], main, NT, preferred_element_type=F32)
        total += lax.dot_general(basis[half, :, 1024:1152], prior, NT, preferred_element_type=F32)
        total = total * alive_row
        acc[pl.ds(s0, 256, stride=SUBS), :] = total[:, 0:128]
        acc[pl.ds(s0 + 1, 256, stride=SUBS), :] = total[:, 128:256]

    def pack(half, r):
        def one(i, carry):
            re = acc[pl.ds(pl.multiple_of((r * 64 + i) * SUBS, SUBS), SUBS), :].astype(BF16)
            im = acc[pl.ds(pl.multiple_of((r * 64 + 32 + i) * SUBS, SUBS), SUBS), :].astype(BF16)
            if half == 1 and r == 0:
                own[0, i, 0:SUBS, 0:128] = re
                own[0, i, 0:SUBS, 128:256] = im
            else:
                sp[half, r, i, :, 0:128] = re
                sp[half, r, i, :, 128:256] = im
            return carry

        lax.fori_loop(0, SHARE, one, 0, unroll=4)

    def transform_rest(half):
        def step(p, carry):
            transform(half, p)
            return carry

        lax.fori_loop(1, 16, step, 0)

    def x_copy(half, r, j):
        src = sp.at[half, r, pl.ds(PER * j, PER)]
        rows = pl.ds((3 - r) * SUBS, SUBS)
        if half == 0:
            dst = swp.at[pl.ds(PER * j, PER), rows, :]
        else:
            dst = own.at[0, pl.ds(PER * j, PER), pl.ds((4 - r) * SUBS, SUBS), :]
        return remote(("x", half, r, j), src, dst, dev(r, 0, 0, c))

    def swap_src(piece):
        return sp.at[0, 0] if piece == "own" else peers(swp, piece)

    def relay_buf(piece):
        return rly if piece == "own" else peers(rlp, piece)

    def turn(piece):
        return -2 if piece == 3 else 2

    def swap_even(piece):
        return remote(("relay", piece), swap_src(piece), relay_buf(piece), dev(0, 0, turn(piece), 0))

    def swap_even_on(piece):
        return remote(("swap", piece), relay_buf(piece), part(own.at[1], piece), dev(0, 0, turn(piece), 0))

    def swap_odd(piece):
        return remote(("far", piece), swap_src(piece), part(pb0.at[1], piece), swap_to)

    def swap_odd_on(piece):
        src, dst = part(pb0.at[1], piece), part(own.at[1], piece)
        return remote(("swap", piece), src, dst, dev(0, 0, -1, 1), ("pass", piece))

    def swap_odd_last(piece):
        return remote(("swap", piece), swap_src(piece), part(own.at[1], piece), dev(0, 0, 4, 1))

    def near_odd(piece):
        return remote(("near", piece), part(own.at[0], piece), part(pb0.at[0], piece), near_to)

    def near_even(piece):
        return remote(("near", piece), part(own.at[0], piece), part(pb0.at[0], piece), dev(0, 0, 0, 1))

    def far_even(piece):
        return remote(("far", piece), part(own.at[1], piece), part(pb0.at[1], piece), dev(0, 0, 0, 1))

    def y_copy(slot, piece):
        name = ("ynear" if slot == 0 else "yfar", piece)
        return remote(name, part(own.at[slot], piece), part(pb1.at[slot], piece), dev(0, 2, 0, c))

    even, odd = c == 0, c == 1

    def send_swap(piece):
        @pl.when(even)
        def _():
            swap_even(piece).start()

        @pl.when(odd)
        def _():
            swap_odd(piece).start()

            @pl.when(zl == 3)
            def _():
                swap_odd_last(piece).start()

    def send_near(piece):
        y_copy(0, piece).start()

        @pl.when(even)
        def _():
            near_even(piece).start()

    def send_near_odd(piece):
        @pl.when(odd)
        def _():
            near_odd(piece).start()

    def pass_on(piece):
        @pl.when(even)
        def _():
            swap_even(piece).wait_recv()
            swap_even_on(piece).start()
            swap_odd(piece).wait_recv()

            @pl.when(zl != 0)
            def _():
                swap_odd_on(piece).start()

    def send_far(piece):
        swap_even_on(piece).wait_recv()
        y_copy(1, piece).start()

        @pl.when(even)
        def _():
            far_even(piece).start()

    def x_done(half, j):
        for r in (1, 2, 3):
            x_copy(half, r, j).wait_recv()

    transform_rest(0)
    tail.wait_recv()

    @pl.when(win == 0)
    def _():
        ts[0, :, 896:1024] = jnp.zeros((CH, 128), BF16)

    transform(0, 0)
    pack(0, 0)
    send_swap("own")
    for r in (1, 2, 3):
        pack(0, r)
    for j in (0, 1):
        for r in (1, 2, 3):
            x_copy(0, r, j).start()
    transform_rest(1)
    transform(1, 0)
    pack(1, 0)
    send_near("own")
    for r in (1, 2, 3):
        pack(1, r)
    for half, j in ((1, 0), (0, 2), (1, 1), (0, 3), (1, 2), (1, 3)):
        for r in (1, 2, 3):
            x_copy(half, r, j).start()

    def stage_x(j):
        x_done(0, j)
        send_swap(j)
        x_done(1, j)
        send_near(j)

    norm = 1.0 / math.sqrt(SUBS * 8)

    def out_copy(j):
        bins = pl.ds(PER * j, PER)
        return pltpu.make_async_copy(outv.at[:, :, bins], out.at[:, :, bins], out_sem.at[j])

    def cross(j):
        for piece in ([j] if j else ["own", j]):
            y_copy(0, piece).wait_recv()
            y_copy(1, piece).wait_recv()
            near_even(piece).wait_recv()

            @pl.when(odd)
            def _():
                far_even(piece).wait_recv()

        def one(i, carry):
            f = PER * j + i
            mine = jnp.concatenate([own[0, f], own[1, f]], axis=0)
            for rnd, ref in ((0, pb0), (1, pb1)):
                other = jnp.concatenate([ref[0, f], ref[1, f]], axis=0)
                g = lax.dot_general(mine, other, TN, preferred_element_type=F32)
                re = (g[0:128, 0:128] + g[128:256, 128:256]) * norm
                im = (g[128:256, 0:128] - g[0:128, 128:256]) * norm
                outv[0, rnd, f] = re.astype(BF16)
                outv[1, rnd, f] = im.astype(BF16)
            return carry

        lax.fori_loop(0, PER, one, 0)
        out_copy(j).start()

    stage_x(0)
    stage_x(1)
    pass_on("own")
    stage_x(2)
    pass_on(0)
    send_far("own")
    stage_x(3)
    pass_on(1)
    send_far(0)
    send_near_odd("own")
    send_near_odd(0)
    pass_on(2)
    send_far(1)
    send_near_odd(1)
    cross(0)
    pass_on(3)
    send_far(2)
    send_near_odd(2)
    cross(1)
    send_far(3)
    send_near_odd(3)
    cross(2)
    cross(3)

    tail.wait_send()
    for half in (0, 1):
        for j in range(CHUNKS):
            for r in (1, 2, 3):
                x_copy(half, r, j).wait_send()
    for piece in PIECES:
        y_copy(0, piece).wait_send()
        y_copy(1, piece).wait_send()

        @pl.when(even)
        def _():
            swap_even(piece).wait_send()
            swap_even_on(piece).wait_send()
            near_even(piece).wait_send()
            far_even(piece).wait_send()

            @pl.when(zl != 0)
            def _():
                swap_odd_on(piece).wait_send()

        @pl.when(odd)
        def _():
            swap_odd(piece).wait_send()
            near_odd(piece).wait_send()

            @pl.when(zl == 3)
            def _():
                swap_odd_last(piece).wait_send()
    for j in range(CHUNKS):
        out_copy(j).wait()


def per_device(traces, taps, alive):
    cos, sin = tables()
    tap_row = jnp.pad(taps.astype(F32)[None, :], ((0, 0), (0, 128 - TAPS)))
    alive_row = alive.astype(F32)[None, :]
    n = len(SEMS)
    vmem = pl.BlockSpec(memory_space=pltpu.VMEM)
    hbm = pl.BlockSpec(memory_space=pl.ANY)
    half = (SHARE, 4 * SUBS, 256)
    return pl.pallas_call(
        kernel,
        out_shape=jax.ShapeDtypeStruct((2, 2, SHARE, CH, CH), BF16),
        in_specs=[hbm, vmem, vmem, hbm, hbm, vmem],
        out_specs=hbm,
        scratch_shapes=[
            pltpu.VMEM((CH, SUBS, SAMPLES), BF16),
            pltpu.VMEM((SUBS + 1, CH, SAMPLES), BF16),
            pltpu.VMEM((BINS, SAMPLES), F32),
            pltpu.VMEM((BINS, SAMPLES), F32),
            pltpu.VMEM((2, 256, SAMPLES + 128), BF16),
            pltpu.VMEM((256 * SUBS, 128), F32),
            pltpu.VMEM((2, 4, SHARE, SUBS, 256), BF16),
            pltpu.VMEM((2,) + half, BF16),
            pltpu.VMEM((2,) + half, BF16),
            pltpu.VMEM((2,) + half, BF16),
            pltpu.VMEM((SHARE, 3 * SUBS, 256), BF16),
            pltpu.VMEM((SHARE, SUBS, 256), BF16),
            pltpu.VMEM((SHARE, 3 * SUBS, 256), BF16),
            pltpu.VMEM((2, 2, SHARE, CH, CH), BF16),
            pltpu.SemaphoreType.DMA((10,)),
            pltpu.SemaphoreType.DMA((CHUNKS,)),
            pltpu.SemaphoreType.DMA((n,)),
            pltpu.SemaphoreType.DMA((n,)),
        ],
        compiler_params=pltpu.CompilerParams(
            collective_id=0, has_side_effects=True, vmem_limit_bytes=60 * 2**20
        ),
        cost_estimate=pl.CostEstimate(flops=7 * 10**9, bytes_accessed=16 * 2**20, transcendentals=0),
    )(traces, tap_row, alive_row, jnp.asarray(cos), jnp.asarray(sin), jnp.asarray(gather_matrix(), BF16))


def solution(mesh):
    return jax.shard_map(
        per_device,
        mesh=mesh,
        in_specs=(P("pair", "win", None), P(), P("pair")),
        out_specs=P(None, None, "win", "pair", None),
        check_vma=False,
    )
```

```python
import math

import jax
import jax.numpy as jnp
import numpy as np
from jax import lax
from jax.experimental import pallas as pl
from jax.experimental.pallas import tpu as pltpu
from jax.sharding import PartitionSpec as P

BINS = 256
SHARE = 32
CH = 128
SUBS = 32
SAMPLES = 1024
TAPS = 64
CHUNKS = 4
PER = SHARE // CHUNKS
MESH = pl.DeviceIdType.MESH
F32 = jnp.float32
BF16 = jnp.bfloat16
NT = (((1,), (1,)), ((), ()))
TN = (((0,), (0,)), ((), ()))


def tables():
    k = np.arange(BINS)[:, None]
    n = np.arange(SAMPLES)[None, :]
    phase = ((k * n) % SAMPLES) * (2.0 * math.pi / SAMPLES)
    return np.cos(phase).astype(np.float32), np.sin(phase).astype(np.float32)


def gather_matrix():
    m = np.zeros((256, 256), np.float32)
    for s in range(16):
        for ch in range(16):
            m[s * 16 + ch, ch * 16 + s] = 1.0
    return m


PIECES = ["own", 0, 1, 2, 3]
STEERED = 3


def part(ref, piece):
    if piece == "own":
        return ref.at[:, pl.ds(0, SUBS), :]
    return ref.at[pl.ds(PER * piece, PER), pl.ds(SUBS, 3 * SUBS), :]


def peers(ref, piece):
    return ref.at[pl.ds(PER * piece, PER)]


def sem_table():
    names = ["tail"]
    names += [("x", half, r, j) for half in (0, 1) for j in range(CHUNKS) for r in (1, 2, 3)]
    for kind in ("swap", "relay", "pass", "near", "far", "ynear", "yfar", "yrelay", "last"):
        names += [(kind, piece) for piece in PIECES]
    return {name: i for i, name in enumerate(names)}


SEMS = sem_table()


def kernel(
    traces, taps, alive, cos_hbm, sin_hbm, perm, out,
    tv, ts, cosv, sinv, basis, acc, sp, own, pb0, pb1, swp, rly, rlp, outv, yrest,
    load_sem, out_sem, send_sem, recv_sem,
):
    pair, win = lax.axis_index("pair"), lax.axis_index("win")
    c, zl, y = lax.rem(pair, 2), lax.rem(pair // 2, 4), pair // 8
    x, hz = win // 2, lax.rem(win, 2)
    z = hz * 4 + zl

    def dev(dx, dy, dz, core):
        xx, yy, zz = lax.rem(x + dx + 4, 4), lax.rem(y + dy + 4, 4), lax.rem(z + dz + 8, 8)
        return {"pair": (yy * 4 + lax.rem(zz, 4)) * 2 + core, "win": xx * 2 + zz // 4}

    next_win = {"pair": pair, "win": lax.rem(win + 1, 8)}
    prev_win = {"pair": pair, "win": lax.rem(win + 7, 8)}
    barrier = pltpu.get_barrier_semaphore()
    side = 2 * c - 1
    same = [dev(r, 0, 0, c) for r in (1, 2, 3)] + [next_win, prev_win]
    same += [dev(0, 2, 0, c), dev(0, 0, 0, 1 - c)]
    same += [dev(0, 1, 0, c), dev(0, -1, 0, c)]
    same += [dev(0, 0, -3 * side, 1 - c), dev(0, 0, side, 1 - c)]
    same += [dev(0, side, side, 1 - c), dev(0, side, 0, 1 - c), dev(0, 0, 3, c), dev(0, 0, -3, c)]
    for target in same:
        pl.semaphore_signal(barrier, inc=1, device_id=target, device_id_type=MESH)

    copies = [
        pltpu.make_async_copy(cos_hbm, cosv, load_sem.at[8]),
        pltpu.make_async_copy(sin_hbm, sinv, load_sem.at[9]),
    ]
    for copy in copies:
        copy.start()

    def load(g):
        rows = pl.ds(pl.multiple_of(g * 16, 16), 16)
        return pltpu.make_async_copy(traces.at[rows], tv.at[rows], load_sem.at[g])

    for g in range(8):
        load(g).start()
    for copy in copies:
        copy.wait()

    scale = 1.0 / math.sqrt(SAMPLES)
    tap_row = jnp.concatenate([taps[0:1, :], jnp.zeros((1, 128 - TAPS), F32)], axis=1)
    lanes = lax.broadcasted_iota(jnp.int32, (128, 128), 1)
    rows = lax.broadcasted_iota(jnp.int32, (128, 128), 0)
    turned = pltpu.roll(jnp.broadcast_to(tap_row, (128, 128)), 0, 1, stride=1, stride_axis=0)
    edge = jnp.where((rows >= TAPS) & (lanes < rows - TAPS), turned, 0.0)
    for half in (0, 1):
        h = hz if half else 1 - hz
        for r in range(4):
            k0 = pl.multiple_of(SHARE * (2 * lax.rem(x + r, 4) + h), SHARE)
            head_cos = cosv[pl.ds(k0, SHARE), 0:128]
            head_sin = sinv[pl.ds(k0, SHARE), 0:128]
            hr = jnp.sum(head_cos * tap_row, axis=1, keepdims=True) * scale
            hi = -jnp.sum(head_sin * tap_row, axis=1, keepdims=True) * scale
            left_re = lax.dot_general(
                head_cos * scale, edge, NT, precision=lax.Precision.HIGHEST, preferred_element_type=F32
            )
            left_im = lax.dot_general(
                head_sin * -scale, edge, NT, precision=lax.Precision.HIGHEST, preferred_element_type=F32
            )
            for t in range(8):
                cs = cosv[pl.ds(k0, SHARE), 128 * t : 128 * t + 128]
                sn = sinv[pl.ds(k0, SHARE), 128 * t : 128 * t + 128]
                re = cs * hr + sn * hi
                im = cs * hi - sn * hr
                if t == 7:
                    re = re - left_re
                    im = im - left_im
                basis[half, 64 * r : 64 * r + 32, 128 * t : 128 * t + 128] = re.astype(BF16)
                basis[half, 64 * r + 32 : 64 * r + 64, 128 * t : 128 * t + 128] = im.astype(BF16)
            basis[half, 64 * r : 64 * r + 32, 1024:1152] = left_re.astype(BF16)
            basis[half, 64 * r + 32 : 64 * r + 64, 1024:1152] = left_im.astype(BF16)

    def regroup(g, carry):
        load(g).wait()
        chans = pl.ds(pl.multiple_of(g * 16, 16), 16)
        for sh in (0, 1):
            for t in range(4):
                cols = slice(256 * t, 256 * t + 256)
                block = tv[chans, 16 * sh : 16 * sh + 16, cols].reshape(256, 256)
                moved = jnp.dot(perm[...], block, preferred_element_type=F32).astype(BF16)
                ts[pl.ds(1 + 16 * sh, 16), chans, cols] = moved.reshape(16, 16, 256)
        return carry

    lax.fori_loop(0, 8, regroup, 0)

    pl.semaphore_wait(barrier, 15)

    def remote(name, src, dst, target, sent=None):
        return pltpu.make_async_remote_copy(
            src_ref=src, dst_ref=dst, send_sem=send_sem.at[SEMS[sent or name]], recv_sem=recv_sem.at[SEMS[name]],
            device_id=target, device_id_type=MESH,
        )

    tail = remote("tail", ts.at[SUBS, :, pl.ds(896, 128)], ts.at[0, :, pl.ds(896, 128)], next_win)
    tail.start()

    alive_row = alive[0:1, :].astype(F32)
    alive_row = jnp.concatenate([alive_row, alive_row], axis=1)

    def transform(half, p):
        s0 = p * 2
        main = ts[pl.ds(s0 + 1, 2)].reshape(256, SAMPLES)
        prior = ts[pl.ds(s0, 2), :, 896:1024].reshape(256, 128)
        total = lax.dot_general(basis[half, :, 0:1024], main, NT, preferred_element_type=F32)
        total += lax.dot_general(basis[half, :, 1024:1152], prior, NT, preferred_element_type=F32)
        total = total * alive_row
        acc[pl.ds(s0, 256, stride=SUBS), :] = total[:, 0:128]
        acc[pl.ds(s0 + 1, 256, stride=SUBS), :] = total[:, 128:256]

    def pack(half, r):
        def one(i, carry):
            re = acc[pl.ds(pl.multiple_of((r * 64 + i) * SUBS, SUBS), SUBS), :].astype(BF16)
            im = acc[pl.ds(pl.multiple_of((r * 64 + 32 + i) * SUBS, SUBS), SUBS), :].astype(BF16)
            if half == 1 and r == 0:
                own[0, i, 0:SUBS, 0:128] = re
                own[0, i, 0:SUBS, 128:256] = im
            else:
                sp[half, r, i, :, 0:128] = re
                sp[half, r, i, :, 128:256] = im
            return carry

        lax.fori_loop(0, SHARE, one, 0, unroll=4)

    def transform_rest(half):
        def step(p, carry):
            transform(half, p)
            return carry

        lax.fori_loop(1, 16, step, 0)

    def x_copy(half, r, j):
        src = sp.at[half, r, pl.ds(PER * j, PER)]
        rows = pl.ds((3 - r) * SUBS, SUBS)
        if half == 0:
            dst = swp.at[pl.ds(PER * j, PER), rows, :]
        else:
            dst = own.at[0, pl.ds(PER * j, PER), pl.ds((4 - r) * SUBS, SUBS), :]
        return remote(("x", half, r, j), src, dst, dev(r, 0, 0, c))

    def swap_src(piece):
        return sp.at[0, 0] if piece == "own" else peers(swp, piece)

    def relay_buf(piece):
        return rly if piece == "own" else peers(rlp, piece)

    def swap_even(piece):
        return remote(("relay", piece), swap_src(piece), relay_buf(piece), dev(0, 0, 3, 1))

    def swap_even_on(piece):
        return remote(("swap", piece), relay_buf(piece), part(own.at[1], piece), dev(0, 0, 1, 0), ("relay", piece))

    def swap_odd(piece):
        return remote(("far", piece), swap_src(piece), part(pb0.at[1], piece), dev(0, 0, -3, 0))

    def swap_odd_on(piece):
        src, dst = part(pb0.at[1], piece), part(own.at[1], piece)
        return remote(("swap", piece), src, dst, dev(0, 0, -1, 1), ("pass", piece))

    def swap_last(piece):
        return remote(("relay", piece), swap_src(piece), relay_buf(piece), dev(0, 0, -3, 0), ("far", piece))

    def swap_last_on(piece):
        src, dst = relay_buf(piece), part(own.at[1], piece)
        return remote(("swap", piece), src, dst, dev(0, 0, -1, 1), ("pass", piece))

    def far_last(piece):
        src, dst = swap_src(piece), part(pb0.at[1], piece)
        return remote(("far", piece), src, dst, dev(0, 1, 1, 0), ("swap", piece))

    def near_odd(piece):
        return remote(("near", piece), part(own.at[0], piece), part(pb0.at[0], piece), dev(0, 0, 1, 0))

    def near_last(piece):
        src = part(own.at[0], piece)
        return remote(("relay", piece), src, relay_buf(piece), dev(0, 1, 0, 0), ("near", piece))

    def near_last_on(piece):
        src, dst = relay_buf(piece), part(pb0.at[0], piece)
        return remote(("near", piece), src, dst, dev(0, 0, -3, 0), ("last", piece))

    def near_even(piece):
        return remote(("near", piece), part(own.at[0], piece), part(pb0.at[0], piece), dev(0, 0, 0, 1))

    def far_even(piece):
        return remote(("far", piece), part(own.at[1], piece), part(pb0.at[1], piece), dev(0, 0, 0, 1))

    def y_copy(slot, piece):
        name = ("ynear" if slot == 0 else "yfar", piece)
        return remote(name, part(own.at[slot], piece), part(pb1.at[slot], piece), dev(0, 2, 0, c))

    def y_first(piece):
        return remote(("yrelay", piece), part(own.at[1], piece), yrest, dev(0, -1, 0, c))

    def y_second(piece):
        return remote(("yfar", piece), yrest, part(pb1.at[1], piece), dev(0, -1, 0, c))

    def y_pass(piece):
        y_first(piece).wait_recv()
        y_second(piece).start()

    even, odd = c == 0, c == 1

    def send_swap(piece):
        @pl.when(even)
        def _():
            swap_even(piece).start()

        @pl.when(odd & (zl != 3))
        def _():
            swap_odd(piece).start()

        @pl.when(odd & (zl == 3))
        def _():
            swap_last(piece).start()

    def send_near(piece):
        y_copy(0, piece).start()

        @pl.when(even)
        def _():
            near_even(piece).start()

        @pl.when(odd & (zl == 3))
        def _():
            near_last(piece).start()

    def send_near_odd(piece):
        @pl.when(odd & (zl != 3))
        def _():
            near_odd(piece).start()

        @pl.when(odd & (zl == 3))
        def _():
            far_last(piece).start()

        @pl.when(even & (zl == 3))
        def _():
            near_last(piece).wait_recv()
            near_last_on(piece).start()

    def pass_even(piece):
        @pl.when(odd)
        def _():
            swap_even(piece).wait_recv()
            swap_even_on(piece).start()

    def pass_odd(piece):
        @pl.when(even & (zl != 0))
        def _():
            swap_odd(piece).wait_recv()
            swap_odd_on(piece).start()

        @pl.when(even & (zl == 0))
        def _():
            swap_last(piece).wait_recv()
            swap_last_on(piece).start()

    def pass_on(piece):
        pass_even(piece)
        pass_odd(piece)

    def send_far(piece):
        swap_even_on(piece).wait_recv()
        (y_first(piece) if piece == STEERED else y_copy(1, piece)).start()

        @pl.when(even)
        def _():
            far_even(piece).start()

    def x_done(half, j):
        for r in (1, 2, 3):
            x_copy(half, r, j).wait_recv()

    transform_rest(0)
    tail.wait_recv()

    @pl.when(win == 0)
    def _():
        ts[0, :, 896:1024] = jnp.zeros((CH, 128), BF16)

    transform(0, 0)
    pack(0, 0)
    send_swap("own")
    for r in (1, 2, 3):
        pack(0, r)
    for j in (0, 1):
        for r in (1, 2, 3):
            x_copy(0, r, j).start()
    transform_rest(1)
    transform(1, 0)
    pack(1, 0)
    send_near("own")
    for r in (1, 2, 3):
        pack(1, r)
    for half, j in ((1, 0), (0, 2), (1, 1), (0, 3), (1, 2), (1, 3)):
        for r in (1, 2, 3):
            x_copy(half, r, j).start()

    def ax(j):
        x_done(0, j)
        send_swap(j)

    def bx(j):
        x_done(1, j)
        send_near(j)

    norm = 1.0 / math.sqrt(SUBS * 8)

    def out_copy(j):
        bins = pl.ds(PER * j, PER)
        return pltpu.make_async_copy(outv.at[:, :, bins], out.at[:, :, bins], out_sem.at[j])

    def cross(j):
        for piece in ([j] if j else ["own", j]):
            y_copy(0, piece).wait_recv()
            y_copy(1, piece).wait_recv()
            near_even(piece).wait_recv()

            @pl.when(odd | (zl == 0))
            def _():
                far_even(piece).wait_recv()

        def one(i, carry):
            f = PER * j + i
            mine = jnp.concatenate([own[0, f], own[1, f]], axis=0)
            for rnd, ref in ((0, pb0), (1, pb1)):
                other = jnp.concatenate([ref[0, f], ref[1, f]], axis=0)
                g = lax.dot_general(mine, other, TN, preferred_element_type=F32)
                re = (g[0:128, 0:128] + g[128:256, 128:256]) * norm
                im = (g[128:256, 0:128] - g[0:128, 128:256]) * norm
                outv[0, rnd, f] = re.astype(BF16)
                outv[1, rnd, f] = im.astype(BF16)
            return carry

        lax.fori_loop(0, PER, one, 0)
        out_copy(j).start()

    ax(0)
    ax(1)
    pass_on('own')
    bx(0)
    ax(2)
    bx(1)
    pass_on(0)
    ax(3)
    bx(2)
    bx(3)
    pass_on(1)
    send_far('own')
    pass_on(2)
    send_far(0)
    pass_on(3)
    send_near_odd('own')
    send_near_odd(0)
    send_near_odd(1)
    send_near_odd(2)
    send_near_odd(3)
    send_far(1)
    send_far(2)
    cross(0)
    send_far(3)
    cross(1)
    y_pass(3)
    cross(2)
    cross(3)

    tail.wait_send()
    for half in (0, 1):
        for j in range(CHUNKS):
            for r in (1, 2, 3):
                x_copy(half, r, j).wait_send()
    for piece in PIECES:
        y_copy(0, piece).wait_send()
        y_copy(1, piece).wait_send()
        if piece == STEERED:
            y_first(piece).wait_send()

        @pl.when(even)
        def _():
            swap_even(piece).wait_send()
            near_even(piece).wait_send()
            far_even(piece).wait_send()

            swap_odd_on(piece).wait_send()

            @pl.when(zl == 3)
            def _():
                near_last_on(piece).wait_send()

        @pl.when(odd)
        def _():
            swap_even_on(piece).wait_send()
            swap_odd(piece).wait_send()
            near_odd(piece).wait_send()

            @pl.when(zl == 3)
            def _():
                far_last(piece).wait_send()
    for j in range(CHUNKS):
        out_copy(j).wait()


def per_device(traces, taps, alive):
    cos, sin = tables()
    n = len(SEMS)
    vmem = pl.BlockSpec(memory_space=pltpu.VMEM)
    hbm = pl.BlockSpec(memory_space=pl.ANY)
    half = (SHARE, 4 * SUBS, 256)
    return pl.pallas_call(
        kernel,
        out_shape=jax.ShapeDtypeStruct((2, 2, SHARE, CH, CH), BF16),
        in_specs=[hbm, vmem, vmem, hbm, hbm, vmem],
        out_specs=hbm,
        scratch_shapes=[
            pltpu.VMEM((CH, SUBS, SAMPLES), BF16),
            pltpu.VMEM((SUBS + 1, CH, SAMPLES), BF16),
            pltpu.VMEM((BINS, SAMPLES), F32),
            pltpu.VMEM((BINS, SAMPLES), F32),
            pltpu.VMEM((2, 256, SAMPLES + 128), BF16),
            pltpu.VMEM((256 * SUBS, 128), F32),
            pltpu.VMEM((2, 4, SHARE, SUBS, 256), BF16),
            pltpu.VMEM((2,) + half, BF16),
            pltpu.VMEM((2,) + half, BF16),
            pltpu.VMEM((2,) + half, BF16),
            pltpu.VMEM((SHARE, 3 * SUBS, 256), BF16),
            pltpu.VMEM((SHARE, SUBS, 256), BF16),
            pltpu.VMEM((SHARE, 3 * SUBS, 256), BF16),
            pltpu.VMEM((2, 2, SHARE, CH, CH), BF16),
            pltpu.VMEM((PER, 3 * SUBS, 256), BF16),
            pltpu.SemaphoreType.DMA((10,)),
            pltpu.SemaphoreType.DMA((CHUNKS,)),
            pltpu.SemaphoreType.DMA((n,)),
            pltpu.SemaphoreType.DMA((n,)),
        ],
        compiler_params=pltpu.CompilerParams(
            collective_id=0, has_side_effects=True, vmem_limit_bytes=60 * 2**20
        ),
        cost_estimate=pl.CostEstimate(flops=7 * 10**9, bytes_accessed=16 * 2**20, transcendentals=0),
    )(traces, taps[None, :], alive[None, :], jnp.asarray(cos), jnp.asarray(sin), jnp.asarray(gather_matrix(), BF16))


def solution(mesh):
    return jax.shard_map(
        per_device,
        mesh=mesh,
        in_specs=(P("pair", "win", None), P(), P("pair")),
        out_specs=P(None, None, "win", "pair", None),
        check_vma=False,
    )
```

```python
import math

import jax
import jax.numpy as jnp
import numpy as np
from jax import lax
from jax.experimental import pallas as pl
from jax.experimental.pallas import tpu as pltpu
from jax.sharding import PartitionSpec as P

BINS = 256
SHARE = 32
CH = 128
SUBS = 32
SAMPLES = 1024
TAPS = 64
CHUNKS = 4
PER = SHARE // CHUNKS
MESH = pl.DeviceIdType.MESH
F32 = jnp.float32
BF16 = jnp.bfloat16
NT = (((1,), (1,)), ((), ()))
TN = (((0,), (0,)), ((), ()))


def tables():
    k = np.arange(BINS)[:, None]
    n = np.arange(SAMPLES)[None, :]
    phase = ((k * n) % SAMPLES) * (2.0 * math.pi / SAMPLES)
    return np.cos(phase).astype(np.float32), np.sin(phase).astype(np.float32)


def gather_matrix():
    m = np.zeros((256, 256), np.float32)
    for s in range(16):
        for ch in range(16):
            m[s * 16 + ch, ch * 16 + s] = 1.0
    return m


PIECES = ["own", 0, 1, 2, 3]
STEERED = 2


def part(ref, piece):
    if piece == "own":
        return ref.at[:, pl.ds(0, SUBS), :]
    return ref.at[pl.ds(PER * piece, PER), pl.ds(SUBS, 3 * SUBS), :]


def peers(ref, piece):
    return ref.at[pl.ds(PER * piece, PER)]


def sem_table():
    names = ["tail"]
    names += [("x", half, r, j) for half in (0, 1) for j in range(CHUNKS) for r in (1, 2, 3)]
    for kind in ("swap", "relay", "pass", "near", "far", "ynear", "yfar", "yrelay", "last"):
        names += [(kind, piece) for piece in PIECES]
    return {name: i for i, name in enumerate(names)}


SEMS = sem_table()


def kernel(
    traces, taps, alive, cos_hbm, sin_hbm, perm, out_re, out_im,
    tv, ts, cosv, sinv, basis, acc, sp, own, pb0, pb1, swp, rly, rlp, outv, yrest,
    load_sem, out_sem, send_sem, recv_sem,
):
    pair, win = lax.axis_index("pair"), lax.axis_index("win")
    c, zl, y = lax.rem(pair, 2), lax.rem(pair // 2, 4), pair // 8
    x, hz = win // 2, lax.rem(win, 2)
    z = hz * 4 + zl

    def dev(dx, dy, dz, core):
        xx, yy, zz = lax.rem(x + dx + 4, 4), lax.rem(y + dy + 4, 4), lax.rem(z + dz + 8, 8)
        return {"pair": (yy * 4 + lax.rem(zz, 4)) * 2 + core, "win": xx * 2 + zz // 4}

    next_win = {"pair": pair, "win": lax.rem(win + 1, 8)}
    prev_win = {"pair": pair, "win": lax.rem(win + 7, 8)}
    barrier = pltpu.get_barrier_semaphore()
    side = 2 * c - 1
    same = [dev(r, 0, 0, c) for r in (1, 2, 3)] + [next_win, prev_win]
    same += [dev(0, 2, 0, c), dev(0, 0, 0, 1 - c)]
    same += [dev(0, 1, 0, c), dev(0, -1, 0, c)]
    same += [dev(0, 0, -3 * side, 1 - c), dev(0, 0, side, 1 - c)]
    same += [dev(0, side, side, 1 - c), dev(0, side, 0, 1 - c), dev(0, 0, 3, c), dev(0, 0, -3, c)]
    for target in same:
        pl.semaphore_signal(barrier, inc=1, device_id=target, device_id_type=MESH)

    copies = [
        pltpu.make_async_copy(cos_hbm, cosv, load_sem.at[8]),
        pltpu.make_async_copy(sin_hbm, sinv, load_sem.at[9]),
    ]
    for copy in copies:
        copy.start()

    def load(g):
        rows = pl.ds(pl.multiple_of(g * 16, 16), 16)
        return pltpu.make_async_copy(traces.at[rows], tv.at[rows], load_sem.at[g])

    for g in range(8):
        load(g).start()
    for copy in copies:
        copy.wait()

    scale = 1.0 / math.sqrt(SAMPLES)
    tap_row = jnp.concatenate([taps[0:1, :], jnp.zeros((1, 128 - TAPS), F32)], axis=1)
    lanes = lax.broadcasted_iota(jnp.int32, (128, 128), 1)
    rows = lax.broadcasted_iota(jnp.int32, (128, 128), 0)
    turned = pltpu.roll(jnp.broadcast_to(tap_row, (128, 128)), 0, 1, stride=1, stride_axis=0)
    edge = jnp.where((rows >= TAPS) & (lanes < rows - TAPS), turned, 0.0)
    for half in (0, 1):
        h = hz if half else 1 - hz
        for r in range(4):
            k0 = pl.multiple_of(SHARE * (2 * lax.rem(x + r, 4) + h), SHARE)
            head_cos = cosv[pl.ds(k0, SHARE), 0:128]
            head_sin = sinv[pl.ds(k0, SHARE), 0:128]
            hr = jnp.sum(head_cos * tap_row, axis=1, keepdims=True) * scale
            hi = -jnp.sum(head_sin * tap_row, axis=1, keepdims=True) * scale
            left_re = lax.dot_general(
                head_cos * scale, edge, NT, precision=lax.Precision.HIGHEST, preferred_element_type=F32
            )
            left_im = lax.dot_general(
                head_sin * -scale, edge, NT, precision=lax.Precision.HIGHEST, preferred_element_type=F32
            )
            for t in range(8):
                cs = cosv[pl.ds(k0, SHARE), 128 * t : 128 * t + 128]
                sn = sinv[pl.ds(k0, SHARE), 128 * t : 128 * t + 128]
                re = cs * hr + sn * hi
                im = cs * hi - sn * hr
                if t == 7:
                    re = re - left_re
                    im = im - left_im
                basis[half, 64 * r : 64 * r + 32, 128 * t : 128 * t + 128] = re.astype(BF16)
                basis[half, 64 * r + 32 : 64 * r + 64, 128 * t : 128 * t + 128] = im.astype(BF16)
            basis[half, 64 * r : 64 * r + 32, 1024:1152] = left_re.astype(BF16)
            basis[half, 64 * r + 32 : 64 * r + 64, 1024:1152] = left_im.astype(BF16)

    def regroup(g, carry):
        load(g).wait()
        chans = pl.ds(pl.multiple_of(g * 16, 16), 16)
        for sh in (0, 1):
            for t in range(4):
                cols = slice(256 * t, 256 * t + 256)
                block = tv[chans, 16 * sh : 16 * sh + 16, cols].reshape(256, 256)
                moved = jnp.dot(perm[...], block, preferred_element_type=F32).astype(BF16)
                ts[pl.ds(1 + 16 * sh, 16), chans, cols] = moved.reshape(16, 16, 256)
        return carry

    lax.fori_loop(0, 8, regroup, 0)

    pl.semaphore_wait(barrier, 15)

    def remote(name, src, dst, target, sent=None):
        return pltpu.make_async_remote_copy(
            src_ref=src, dst_ref=dst, send_sem=send_sem.at[SEMS[sent or name]], recv_sem=recv_sem.at[SEMS[name]],
            device_id=target, device_id_type=MESH,
        )

    tail = remote("tail", ts.at[SUBS, :, pl.ds(896, 128)], ts.at[0, :, pl.ds(896, 128)], next_win)
    tail.start()

    alive_row = alive[0:1, :].astype(F32)
    alive_row = jnp.concatenate([alive_row, alive_row], axis=1)

    def transform(half, p):
        s0 = p * 2
        main = ts[pl.ds(s0 + 1, 2)].reshape(256, SAMPLES)
        prior = ts[pl.ds(s0, 2), :, 896:1024].reshape(256, 128)
        total = lax.dot_general(basis[half, :, 0:1024], main, NT, preferred_element_type=F32)
        total += lax.dot_general(basis[half, :, 1024:1152], prior, NT, preferred_element_type=F32)
        total = total * alive_row
        acc[pl.ds(s0, 256, stride=SUBS), :] = total[:, 0:128]
        acc[pl.ds(s0 + 1, 256, stride=SUBS), :] = total[:, 128:256]

    def pack(half, r):
        def one(i, carry):
            re = acc[pl.ds(pl.multiple_of((r * 64 + i) * SUBS, SUBS), SUBS), :].astype(BF16)
            im = acc[pl.ds(pl.multiple_of((r * 64 + 32 + i) * SUBS, SUBS), SUBS), :].astype(BF16)
            if half == 1 and r == 0:
                own[0, i, 0:SUBS, 0:128] = re
                own[0, i, 0:SUBS, 128:256] = im
            else:
                sp[half, r, i, :, 0:128] = re
                sp[half, r, i, :, 128:256] = im
            return carry

        lax.fori_loop(0, SHARE, one, 0, unroll=16)

    def transform_rest(half):
        def step(p, carry):
            transform(half, p)
            return carry

        lax.fori_loop(1, 16, step, 0)

    def x_copy(half, r, j):
        src = sp.at[half, r, pl.ds(PER * j, PER)]
        rows = pl.ds((3 - r) * SUBS, SUBS)
        if half == 0:
            dst = swp.at[pl.ds(PER * j, PER), rows, :]
        else:
            dst = own.at[0, pl.ds(PER * j, PER), pl.ds((4 - r) * SUBS, SUBS), :]
        return remote(("x", half, r, j), src, dst, dev(r, 0, 0, c))

    def swap_src(piece):
        return sp.at[0, 0] if piece == "own" else peers(swp, piece)

    def relay_buf(piece):
        return rly if piece == "own" else peers(rlp, piece)

    def swap_even(piece):
        return remote(("relay", piece), swap_src(piece), relay_buf(piece), dev(0, 0, 3, 1))

    def swap_even_on(piece):
        return remote(("swap", piece), relay_buf(piece), part(own.at[1], piece), dev(0, 0, 1, 0), ("relay", piece))

    def swap_odd(piece):
        return remote(("far", piece), swap_src(piece), part(pb0.at[1], piece), dev(0, 0, -3, 0))

    def swap_odd_on(piece):
        src, dst = part(pb0.at[1], piece), part(own.at[1], piece)
        return remote(("swap", piece), src, dst, dev(0, 0, -1, 1), ("pass", piece))

    def swap_last(piece):
        return remote(("relay", piece), swap_src(piece), relay_buf(piece), dev(0, 0, -3, 0), ("far", piece))

    def swap_last_on(piece):
        src, dst = relay_buf(piece), part(own.at[1], piece)
        return remote(("swap", piece), src, dst, dev(0, 0, -1, 1), ("pass", piece))

    def far_last(piece):
        src, dst = swap_src(piece), part(pb0.at[1], piece)
        return remote(("far", piece), src, dst, dev(0, 1, 1, 0), ("swap", piece))

    def near_odd(piece):
        return remote(("near", piece), part(own.at[0], piece), part(pb0.at[0], piece), dev(0, 0, 1, 0))

    def near_last(piece):
        src = part(own.at[0], piece)
        return remote(("relay", piece), src, relay_buf(piece), dev(0, 1, 0, 0), ("near", piece))

    def near_last_on(piece):
        src, dst = relay_buf(piece), part(pb0.at[0], piece)
        return remote(("near", piece), src, dst, dev(0, 0, -3, 0), ("last", piece))

    def near_even(piece):
        return remote(("near", piece), part(own.at[0], piece), part(pb0.at[0], piece), dev(0, 0, 0, 1))

    def far_even(piece):
        return remote(("far", piece), part(own.at[1], piece), part(pb0.at[1], piece), dev(0, 0, 0, 1))

    def y_copy(slot, piece):
        name = ("ynear" if slot == 0 else "yfar", piece)
        return remote(name, part(own.at[slot], piece), part(pb1.at[slot], piece), dev(0, 2, 0, c))

    def y_first(piece):
        return remote(("yrelay", piece), part(own.at[1], piece), yrest, dev(0, -1, 0, c))

    def y_second(piece):
        return remote(("yfar", piece), yrest, part(pb1.at[1], piece), dev(0, -1, 0, c))

    def y_pass(piece):
        y_first(piece).wait_recv()
        y_second(piece).start()

    even, odd = c == 0, c == 1

    def send_swap(piece):
        @pl.when(even)
        def _():
            swap_even(piece).start()

        @pl.when(odd & (zl != 3))
        def _():
            swap_odd(piece).start()

        @pl.when(odd & (zl == 3))
        def _():
            swap_last(piece).start()

    def send_near(piece):
        y_copy(0, piece).start()

        @pl.when(even)
        def _():
            near_even(piece).start()

        @pl.when(odd & (zl == 3))
        def _():
            near_last(piece).start()

    def send_near_odd(piece):
        @pl.when(odd & (zl != 3))
        def _():
            near_odd(piece).start()

    def send_far_last(piece):
        @pl.when(odd & (zl == 3))
        def _():
            far_last(piece).start()

    def send_near_last(piece):
        @pl.when(even & (zl == 3))
        def _():
            near_last(piece).wait_recv()
            near_last_on(piece).start()

    def pass_even(piece):
        @pl.when(odd)
        def _():
            swap_even(piece).wait_recv()
            swap_even_on(piece).start()

    def pass_odd(piece):
        @pl.when(even & (zl != 0))
        def _():
            swap_odd(piece).wait_recv()
            swap_odd_on(piece).start()

        @pl.when(even & (zl == 0))
        def _():
            swap_last(piece).wait_recv()
            swap_last_on(piece).start()

    def pass_on(piece):
        pass_even(piece)
        pass_odd(piece)

    def send_far(piece):
        swap_even_on(piece).wait_recv()
        (y_first(piece) if piece == STEERED else y_copy(1, piece)).start()

        @pl.when(even)
        def _():
            far_even(piece).start()

    def x_done(half, j):
        for r in (1, 2, 3):
            x_copy(half, r, j).wait_recv()

    transform_rest(0)
    tail.wait_recv()

    @pl.when(win == 0)
    def _():
        ts[0, :, 896:1024] = jnp.zeros((CH, 128), BF16)

    transform(0, 0)
    pack(0, 0)
    send_swap("own")
    for r in (1, 2, 3):
        pack(0, r)
    for j in (0, 1):
        for r in (1, 2, 3):
            x_copy(0, r, j).start()
    transform_rest(1)
    transform(1, 0)
    pack(1, 0)
    send_near("own")
    for r in (1, 2, 3):
        pack(1, r)
    for half, j in ((1, 0), (0, 2), (1, 1), (0, 3), (1, 2), (1, 3)):
        for r in (1, 2, 3):
            x_copy(half, r, j).start()

    def ax(j):
        x_done(0, j)
        send_swap(j)

    def bx(j):
        x_done(1, j)
        send_near(j)

    norm = 1.0 / math.sqrt(SUBS * 8)

    def out_copy(j):
        bins = pl.ds(PER * j, PER)
        return [
            pltpu.make_async_copy(outv.at[k, :, bins], ref.at[:, bins], out_sem.at[j, k])
            for k, ref in ((0, out_re), (1, out_im))
        ]

    def cross(j):
        for piece in ([j] if j else ["own", j]):
            y_copy(0, piece).wait_recv()
            y_copy(1, piece).wait_recv()
            near_even(piece).wait_recv()

            @pl.when(odd | (zl == 0))
            def _():
                far_even(piece).wait_recv()

        def one(i, carry):
            f = PER * j + i
            mine = jnp.concatenate([own[0, f], own[1, f]], axis=0)
            for rnd, ref in ((0, pb0), (1, pb1)):
                other = jnp.concatenate([ref[0, f], ref[1, f]], axis=0)
                g = lax.dot_general(mine, other, TN, preferred_element_type=F32)
                re = (g[0:128, 0:128] + g[128:256, 128:256]) * norm
                im = (g[128:256, 0:128] - g[0:128, 128:256]) * norm
                outv[0, rnd, f] = re.astype(BF16)
                outv[1, rnd, f] = im.astype(BF16)
            return carry

        lax.fori_loop(0, PER, one, 0)
        for copy in out_copy(j):
            copy.start()

    ax(0)
    ax(1)
    pass_on('own')
    bx(0)
    ax(2)
    bx(1)
    pass_on(0)
    ax(3)
    bx(2)
    bx(3)
    pass_on(1)
    send_near_last('own')
    send_far_last('own')
    send_far('own')
    pass_on(2)
    send_near_last(0)
    send_far_last(0)
    send_far(0)
    pass_on(3)
    send_near_last(1)
    send_near_odd('own')
    send_near_odd(0)
    send_near_odd(1)
    send_near_odd(2)
    send_near_odd(3)
    send_far_last(1)
    send_far_last(2)
    send_far_last(3)
    send_far(1)
    send_near_last(2)
    send_far(2)
    send_near_last(3)
    cross(0)
    send_far(3)
    cross(1)
    y_pass(2)
    cross(2)
    cross(3)

    tail.wait_send()
    for half in (0, 1):
        for j in range(CHUNKS):
            for r in (1, 2, 3):
                x_copy(half, r, j).wait_send()
    for piece in PIECES:
        y_copy(0, piece).wait_send()
        y_copy(1, piece).wait_send()
        if piece == STEERED:
            y_first(piece).wait_send()

        @pl.when(even)
        def _():
            swap_even(piece).wait_send()
            near_even(piece).wait_send()
            far_even(piece).wait_send()

            swap_odd_on(piece).wait_send()

            @pl.when(zl == 3)
            def _():
                near_last_on(piece).wait_send()

        @pl.when(odd)
        def _():
            swap_even_on(piece).wait_send()
            swap_odd(piece).wait_send()
            near_odd(piece).wait_send()

            @pl.when(zl == 3)
            def _():
                far_last(piece).wait_send()
    for j in range(CHUNKS):
        for copy in out_copy(j):
            copy.wait()


def per_device(traces, taps, alive):
    cos, sin = tables()
    n = len(SEMS)
    vmem = pl.BlockSpec(memory_space=pltpu.VMEM)
    hbm = pl.BlockSpec(memory_space=pl.ANY)
    half = (SHARE, 4 * SUBS, 256)
    result = jax.ShapeDtypeStruct((2, SHARE, CH, CH), BF16)
    parts = pl.pallas_call(
        kernel,
        out_shape=(result, result),
        in_specs=[hbm, vmem, vmem, hbm, hbm, vmem],
        out_specs=(hbm, hbm),
        scratch_shapes=[
            pltpu.VMEM((CH, SUBS, SAMPLES), BF16),
            pltpu.VMEM((SUBS + 1, CH, SAMPLES), BF16),
            pltpu.VMEM((BINS, SAMPLES), F32),
            pltpu.VMEM((BINS, SAMPLES), F32),
            pltpu.VMEM((2, 256, SAMPLES + 128), BF16),
            pltpu.VMEM((256 * SUBS, 128), F32),
            pltpu.VMEM((2, 4, SHARE, SUBS, 256), BF16),
            pltpu.VMEM((2,) + half, BF16),
            pltpu.VMEM((2,) + half, BF16),
            pltpu.VMEM((2,) + half, BF16),
            pltpu.VMEM((SHARE, 3 * SUBS, 256), BF16),
            pltpu.VMEM((SHARE, SUBS, 256), BF16),
            pltpu.VMEM((SHARE, 3 * SUBS, 256), BF16),
            pltpu.VMEM((2, 2, SHARE, CH, CH), BF16),
            pltpu.VMEM((PER, 3 * SUBS, 256), BF16),
            pltpu.SemaphoreType.DMA((10,)),
            pltpu.SemaphoreType.DMA((CHUNKS, 2)),
            pltpu.SemaphoreType.DMA((n,)),
            pltpu.SemaphoreType.DMA((n,)),
        ],
        compiler_params=pltpu.CompilerParams(
            collective_id=0, has_side_effects=True, vmem_limit_bytes=60 * 2**20
        ),
        cost_estimate=pl.CostEstimate(flops=7 * 10**9, bytes_accessed=16 * 2**20, transcendentals=0),
    )(traces, taps[None, :], alive[None, :], jnp.asarray(cos), jnp.asarray(sin), jnp.asarray(gather_matrix(), BF16))
    return jnp.stack(parts, axis=0)


def solution(mesh):
    return jax.shard_map(
        per_device,
        mesh=mesh,
        in_specs=(P("pair", "win", None), P(), P("pair")),
        out_specs=P(None, None, "win", "pair", None),
        check_vma=False,
    )
```
